32 devices in a mesh: parts: 2 (over y), blk: 4 (over z), reader: 4 (over x, core), sub: 1.
Axes of the slice: x: 2, y: 2, z: 4, core: 2. Of those that a mesh axis runs over, the one named last changes fastest.
Arguments:
- images: bfloat16 [3072, 8192], P(('parts', 'blk', 'reader'), 'sub'), parts along dimension 0, may hold values from -40 to 40
- routes: int32 [3072, 2], P(('parts', 'blk', 'reader')), parts along dimension 0, may hold values from 0 to 3, all different within a row; in each aligned block of 96 rows (0 to 95, 96 to 191, ...) at most 96 rows name the same one
- projections: bfloat16 [8, 128, 8192], P(('parts', 'reader'), 'blk', 'sub'), parts along dimension 0, may hold values from -8 to 8
- noise_weights: float32 [16384], P(('parts', 'sub')), parts along dimension 0, may hold values from 0.3 to 3
Outputs:
- weighted_sums: float32 [8, 128, 8192], P(('parts', 'reader'), 'blk', 'sub'), parts along dimension 0
- normalizer: float32 [3072], P(('parts', 'blk', 'reader')), parts along dimension 0
The draws below stay inside these ranges and needn't reach their ends.
There are 2 independent parts, one for each index of `parts`. The reference program is written for one: setup_inputs(seed, part) draws one part's arguments, and reference() takes and returns one part's arrays. A program takes and returns all parts, laid end to end along the dimension named above; each array names one. Nothing has to cross between parts.
Inputs may be any that keep to these rules, and one draw needn't show every extreme that they name: `routes`: each row names 2 different class groups. In the rows of one device (aligned blocks of 96 rows) no group is named by more than 96 rows, a bound that some block reaches.
All inputs are finite; a program needn't handle non-finite values.
Results may differ from the reference program's by a relative error of at most 0.019.
Values may be sent and summed in bfloat16 or wider, within the bound.
A program may use at most 64 MiB of HBM per device.

```python
import math
import jax
import jax.numpy as jnp
import numpy as np
from jax import lax

COEF = 8192
PART_DEV = 96
TOP = 2
GROUPS = 4
GREFS = 128
CAP = 96
RECV = 384
PARTICLES = 1536
N_BLK = 4
N_READER = 4


def projection_values(key):
    folded = jax.random.fold_in(key, 101)
    scale_key, vector_key = jax.random.split(folded)
    scales = jnp.exp(jax.random.uniform(scale_key, (GROUPS, GREFS, 1), jnp.float32, math.log(0.6), math.log(6.0)))
    vectors = jax.random.truncated_normal(vector_key, -4.0, 4.0, (GROUPS, GREFS, COEF), jnp.float32)
    return jnp.clip(scales * vectors * COEF ** (-0.5), -8.0, 8.0)


def draw_projections(key, part):
    return projection_values(key).astype(jnp.bfloat16)


def draw_images(key, part):
    folded = jax.random.fold_in(key, 202)
    key_list = jax.random.split(folded, 2)
    row_scale = jnp.exp(jax.random.uniform(key_list[0], (PARTICLES, 1), jnp.float32, math.log(0.3), math.log(3.0)))
    values = row_scale * jax.random.truncated_normal(key_list[1], -6.0, 6.0, (PARTICLES, COEF), jnp.float32)
    return jnp.clip(values, -40.0, 40.0).astype(jnp.bfloat16)


def deal_out(rng, own, number, rows, number_of, top, bound, slope):
    ranking = jax.random.permutation(rng, number_of)
    crowded, usual = shares(number_of, rows * top, bound, slope, True), shares(number_of, rows * top, bound, slope, False)
    places = jnp.arange(number_of)

    def named(sizes, rotation):
        used = int((sizes > 0).sum())
        fixed = max(1, used // 4)
        passed = fixed + (places - fixed + rotation * (used - fixed)) % max(1, number_of - fixed)
        return jnp.zeros((number_of,), jnp.int32).at[ranking[jnp.where(places < fixed, places, passed)]].set(jnp.asarray(sizes, jnp.int32))

    sizes = jnp.where(number % 4 == 0, named(crowded, number // 4), named(usual, number - number // 4 - 1))
    mixed = jax.random.permutation(jax.random.fold_in(own, 3), number_of)
    giver, receiver = mixed[0:number_of // 2 * 2:2], mixed[1:number_of // 2 * 2:2]
    slack = jnp.minimum(sizes[giver] - 1, bound - sizes[receiver]) // 2
    slack = jnp.where((giver == ranking[0]) | (receiver == ranking[0]) | (sizes[receiver] == 0), 0, jnp.maximum(slack, 0))
    passed = jax.random.randint(jax.random.fold_in(own, 4), (number_of // 2,), 0, 1 << 20) % (slack + 1)
    sizes = sizes.at[giver].add(-passed).at[receiver].add(passed)
    members = jnp.searchsorted(jnp.cumsum(sizes), jnp.arange(rows * top), side="right").astype(jnp.int32)
    listing = members.reshape(top, rows).T
    listing = listing[jax.random.permutation(jax.random.fold_in(own, 1), rows)]
    rotation = jax.random.randint(jax.random.fold_in(own, 2), (rows, 1), 0, top)
    return jnp.take_along_axis(listing, (jnp.arange(top)[None, :] + rotation) % top, axis=1)


def shares(amount, total, bound, skew, full):
    loads = [(1 << 20) // math.isqrt(rank ** skew) + 1 for rank in range(1, amount + 1)]
    largest = bound if full else min(bound, max(-(-total // amount), total * loads[0] // sum(loads)))
    least = 1 if total - largest >= amount - 1 else 0
    holding, spare = [largest] + [least] * (amount - 1), total - largest - least * (amount - 1)
    while spare > 0:
        movable = [i for i in range(1, amount) if holding[i] < largest] or [i for i in range(1, amount) if holding[i] < bound]
        pool, remaining = sum([loads[i] for i in movable]), spare
        for i in movable:
            extra = min(bound - holding[i], max(1, remaining * loads[i] // pool), spare)
            holding[i] = holding[i] + extra
            spare = spare - extra
    return np.array(holding)


def setup_inputs(seed: int = 0, part: int = 0) -> dict:
    keys = jax.random.split(jax.random.key(seed), 5)
    part_keys = jax.random.split(jax.random.fold_in(keys[4], part), 5)
    images = draw_images(jax.random.fold_in(jax.random.fold_in(keys[4], part), 71), part)
    routes_keys = jax.random.split(jax.random.fold_in(part_keys[1], 1), PARTICLES // PART_DEV)
    routes_turns = jax.random.permutation(jax.random.fold_in(part_keys[1], 3), PARTICLES // PART_DEV)
    routes = jax.vmap(lambda own, number: deal_out(jax.random.fold_in(part_keys[1], 2), own, number, PART_DEV, N_READER, TOP, CAP, 2))(routes_keys, routes_turns).reshape((PARTICLES, TOP))
    projections = draw_projections(jax.random.fold_in(jax.random.fold_in(keys[4], part), 71), part)
    noise_weights = jnp.clip(jnp.exp(jax.random.uniform(part_keys[3], (COEF,), jnp.float32, math.log(0.3), math.log(3.0))), 0.3, 3.0)
    return dict(images=images, routes=routes, projections=projections, noise_weights=noise_weights)


def combine_stats(row_peaks, row_totals):
    highest = jnp.max(row_peaks, axis=-1)
    spread = row_totals * jnp.exp(row_peaks - highest[..., None])
    return highest + jnp.log(jnp.sum(spread, axis=-1))


def reference(images, routes, projections, noise_weights):
    scaled = projections.astype(jnp.float32) * noise_weights[None, None, :]
    weighted = scaled.astype(jnp.bfloat16)
    penalty = 0.5 * jnp.sum(scaled * projections.astype(jnp.float32), axis=2)
    row_count = N_READER * PART_DEV
    image_rows = images.reshape(N_BLK, row_count, COEF)
    route_rows = routes.reshape(N_BLK, row_count, TOP)
    group_numbers = jnp.arange(GROUPS, dtype=jnp.int32)
    row_numbers = jnp.arange(row_count, dtype=jnp.int32)

    def one_row(running, inputs):
        block_images, block_routes = inputs

        def score_group(group_id):
            member = jnp.any(block_routes == group_id, axis=1)
            ordering = jnp.argsort(jnp.where(member, 0, 1).astype(jnp.int32), stable=True)[:RECV].astype(jnp.int32)
            chosen = block_images[ordering]
            scores = jnp.dot(chosen, weighted[group_id].T, preferred_element_type=jnp.float32) - penalty[group_id][None, :]
            row_peak = jnp.max(scores, axis=1)
            row_total = jnp.sum(jnp.exp(scores - row_peak[:, None]), axis=1)
            full_peak = jnp.zeros((row_count,), jnp.float32).at[ordering].set(row_peak)
            full_total = jnp.zeros((row_count,), jnp.float32).at[ordering].set(row_total)
            return scores, ordering, member[ordering], full_peak, full_total

        score_table, order_table, live_table, peak_table, total_table = lax.map(score_group, group_numbers)
        picked_peaks = peak_table[block_routes, row_numbers[:, None]]
        picked_totals = total_table[block_routes, row_numbers[:, None]]
        particle_norm = combine_stats(picked_peaks, picked_totals)

        def back_group(inputs):
            scores, ordering, live_slot = inputs
            slot_norm = particle_norm[ordering]
            exponent = jnp.where(live_slot[:, None], scores - slot_norm[:, None], -jnp.inf)
            posterior = jnp.exp(exponent).astype(jnp.bfloat16)
            chosen = block_images[ordering]
            partial_value = jnp.dot(posterior.T, chosen, preferred_element_type=jnp.float32)
            return partial_value.astype(jnp.bfloat16)

        partials = lax.map(back_group, (score_table, order_table, live_table))
        partials = lax.optimization_barrier(partials)
        return running + partials.astype(jnp.float32), particle_norm

    initial = jnp.zeros((GROUPS, GREFS, COEF), jnp.float32)
    total_sums, norm_rows = lax.scan(one_row, initial, (image_rows, route_rows))
    return total_sums, norm_rows.reshape(PARTICLES)
```

```python
from functools import partial

import jax
import jax.numpy as jnp
from jax import lax
from jax.experimental import pallas as pl
from jax.experimental.pallas import tpu as pltpu
from jax.sharding import PartitionSpec as P

MESH = pl.DeviceIdType.MESH


def from_behind(block, axis, distance):
    devices = range(lax.axis_size(axis))
    route = [((i - distance) % len(devices), i) for i in devices]
    return lax.ppermute(block, axis, route)


def slot_positions(route_block):
    flat = route_block.reshape(-1)
    order = jnp.arange(flat.shape[0], dtype=jnp.int32)
    earlier = (order[None, :] < order[:, None]) & (flat[None, :] == flat[:, None])
    return jnp.sum(earlier.astype(jnp.int32), axis=1).reshape(route_block.shape)


def combine_stats(row_peaks, row_totals):
    highest = jnp.max(row_peaks, axis=-1)
    spread = row_totals * jnp.exp(row_peaks - highest[..., None])
    return highest + jnp.log(jnp.sum(spread, axis=-1))


def routed(images, routes, projections, noise_weights):
    groups = lax.axis_size("reader")
    cycle_size = lax.axis_size("blk")
    my_group = lax.axis_index("reader")
    my_member = lax.axis_index("blk")
    per_device, top_count = routes.shape
    half_width = images.shape[1]
    capacity = min(per_device, 2 * per_device * top_count // groups)
    slot_count = groups * capacity
    ref_count = projections.shape[1]
    all_refs = ref_count * cycle_size
    anchor = jnp.zeros((), jnp.int32)
    own_index = slot_positions(routes)
    own_target = routes * capacity + own_index
    sources = jnp.broadcast_to(jnp.arange(per_device, dtype=jnp.int32)[:, None], routes.shape)
    picker = (
        jnp.full((slot_count,), per_device, jnp.int32)
        .at[own_target.reshape(-1)]
        .set(sources.reshape(-1))
    )
    padded = jnp.concatenate([images, jnp.zeros((1, half_width), images.dtype)], axis=0)
    outgoing = padded[picker].reshape(groups, capacity, half_width)
    received = lax.all_to_all(outgoing, "reader", split_axis=0, concat_axis=0, tiled=True).reshape(
        slot_count, half_width
    )
    every_route = lax.all_gather(routes, "reader", axis=0, tiled=True).reshape(
        groups, per_device, top_count
    )
    every_index = jax.vmap(slot_positions)(every_route)
    senders = jnp.arange(groups, dtype=jnp.int32)[:, None, None]
    landing = jnp.where(every_route == my_group, senders * capacity + every_index, slot_count)
    live_slot = jnp.zeros((slot_count,), jnp.int32).at[landing.reshape(-1)].set(1, mode="drop") > 0

    def score_block(ref_block):
        scaled = ref_block.astype(jnp.float32) * noise_weights[None, :]
        weighted = scaled.astype(jnp.bfloat16)
        penalty = 0.5 * jnp.sum(scaled * ref_block.astype(jnp.float32), axis=1)
        partial_scores = lax.dot_general(
            weighted, received, (((1,), (1,)), ((), ())), preferred_element_type=jnp.float32
        )
        return partial_scores - penalty[:, None]

    def cycle_turn(rotation, carry):
        ref_block, score_table = carry
        position = (my_member - rotation) % cycle_size
        score_table = lax.dynamic_update_slice(
            score_table, score_block(ref_block)[None], (position, anchor, anchor)
        )
        ref_block = from_behind(ref_block, "blk", 1)
        return (ref_block, score_table)

    empty_table = jnp.zeros((cycle_size, ref_count, slot_count), jnp.float32)
    ref_block, score_table = lax.fori_loop(
        0, cycle_size - 1, cycle_turn, (projections[0], empty_table)
    )
    position = (my_member + 1) % cycle_size
    score_table = lax.dynamic_update_slice(
        score_table, score_block(ref_block)[None], (position, anchor, anchor)
    )
    score_table = lax.psum(score_table, "sub")
    scores = score_table.reshape(all_refs, slot_count)
    row_peak = jnp.max(scores, axis=0)
    row_total = jnp.sum(jnp.exp(scores - row_peak[None, :]), axis=0)
    back_peak, back_total = (
        lax.all_to_all(
            row_peak.reshape(groups, capacity), "reader", split_axis=0, concat_axis=0, tiled=True
        ),
        lax.all_to_all(
            row_total.reshape(groups, capacity), "reader", split_axis=0, concat_axis=0, tiled=True
        ),
    )
    normalizer = combine_stats(
        back_peak.reshape(-1)[own_target], back_total.reshape(-1)[own_target]
    )
    outgoing_norm = (
        jnp.zeros((slot_count,), jnp.float32)
        .at[own_target.reshape(-1)]
        .set(jnp.repeat(normalizer, top_count))
    )
    slot_norm = lax.all_to_all(
        outgoing_norm.reshape(groups, capacity), "reader", split_axis=0, concat_axis=0, tiled=True
    ).reshape(slot_count)
    exponent = jnp.where(live_slot[None, :], scores - slot_norm[None, :], -jnp.inf)
    posterior = jnp.exp(exponent).astype(jnp.bfloat16)
    summed = lax.psum_scatter(
        jnp.dot(posterior, received, preferred_element_type=jnp.float32).astype(jnp.bfloat16),
        "blk",
        scatter_dimension=0,
        tiled=True,
    ).astype(jnp.float32)
    return (summed[None], normalizer)


def flipped(number, mask, size):
    result, bit = 0, 1
    while bit < size:
        digit = lax.rem(lax.div(number, bit), 2)
        result = result + bit * ((1 - digit) if mask & bit else digit)
        bit *= 2
    return result


def kernel(
    R, B,
    images, routes, proj, noise,
    out, norm,
    X, PR, S, SR, Q, PART, UR, DR, US, DS, O,
    loc, p_snd, p_rcv, x_snd, x_rcv, gu_snd, gd_snd, s_snd, s_rcv, q_snd, q_rcv,
    u_snd, u_rcv, d_snd, d_rcv, o_snd, o_rcv,
):
    r = lax.axis_index("reader")
    b = lax.axis_index("blk")
    rows = images.shape[0]
    refs = proj.shape[0]
    Cs = X.shape[2]
    width = R * refs
    far = [k for k in range(R - 1, 1, -1)]
    masks = far + [1]
    peers = {k: flipped(r, k, R) for k in masks}
    not_top = b < B - 1
    not_bottom = b > 0

    def span(i):
        return pl.ds(pl.multiple_of(i * Cs, Cs), Cs)

    def to_reader(src, dst, snd, rcv, k):
        return pltpu.make_async_remote_copy(
            src_ref=src, dst_ref=dst, send_sem=snd, recv_sem=rcv,
            device_id={"reader": peers[k]}, device_id_type=MESH,
        )

    def to_blk(src, dst, snd, rcv, step):
        return pltpu.make_async_remote_copy(
            src_ref=src, dst_ref=dst, send_sem=snd, recv_sem=rcv,
            device_id={"blk": b + step}, device_id_type=MESH,
        )

    def proj_copy(k):
        return to_reader(proj.at[:, span(peers[k])], PR.at[b, r], p_snd.at[k], p_rcv.at[b, r], k)

    def image_copy(k):
        return to_reader(images.at[:, span(peers[k])], X.at[r], x_snd.at[k], x_rcv.at[r], k)

    def gather_copy(src, g, step):
        snd = gu_snd if step > 0 else gd_snd
        return to_blk(PR.at[src, g], PR.at[src, g], snd.at[src, g], p_rcv.at[src, g], step)

    def score_copy(src, k):
        return to_reader(S.at[src, peers[k]], SR.at[src, r], s_snd.at[src, k], s_rcv.at[src, r], k)

    def post_copy(k):
        return to_reader(Q.at[:, r], Q.at[:, r], q_snd.at[k], q_rcv.at[r], k)

    def up_copy(d, g):
        return to_blk(US.at[d, g], UR.at[d, g], u_snd.at[d, g], u_rcv.at[d, g], 1)

    def down_copy(d, g):
        return to_blk(DS.at[d, g], DR.at[d, g], d_snd.at[d, g], d_rcv.at[d, g], -1)

    def out_copy(k):
        return to_reader(O.at[k], out.at[:, span(r)], o_snd.at[k], o_rcv.at[r], k)

    def arrived(dst, sem):
        to_reader(dst, dst, sem, sem, 1).wait_recv()

    own_proj = pltpu.make_async_copy(proj.at[:, span(r)], PR.at[b, r], loc.at[0])
    own_image = pltpu.make_async_copy(images.at[:, span(r)], X.at[r], loc.at[1])
    own_proj.start()

    barrier = pltpu.get_barrier_semaphore()
    for k in masks:
        pl.semaphore_signal(barrier, inc=1, device_id={"reader": peers[k]}, device_id_type=MESH)

    @pl.when(not_top)
    def _():
        pl.semaphore_signal(barrier, inc=1, device_id={"blk": b + 1}, device_id_type=MESH)

    @pl.when(not_bottom)
    def _():
        pl.semaphore_signal(barrier, inc=1, device_id={"blk": b - 1}, device_id_type=MESH)

    pl.semaphore_wait(
        barrier, (R - 1) + not_top.astype(jnp.int32) + not_bottom.astype(jnp.int32)
    )

    for k in masks:
        proj_copy(k).start()
    own_proj.wait()

    def send_own(g):
        @pl.when(not_top)
        def _():
            gather_copy(b, g, 1).start()

        @pl.when(not_bottom)
        def _():
            gather_copy(b, g, -1).start()

    send_own(r)
    own_image.start()
    for k in masks:
        image_copy(k).start()
    order = [1] + far[::-1]
    for k in order:
        arrived(PR.at[b, peers[k]], p_rcv.at[b, peers[k]])
        send_own(peers[k])

    tile = min(Cs, 512)

    def score_chunk(src):
        scores = jnp.zeros((R * rows, width), jnp.float32)
        penalty = jnp.zeros((8, width), jnp.float32)
        for t in range(Cs // tile):
            cut = pl.ds(t * tile, tile)
            refs_f = PR[src, :, :, cut].reshape(width, tile).astype(jnp.float32)
            scaled = refs_f * noise[r, :, cut]
            scores = scores + lax.dot_general(
                X[:, :, cut].reshape(R * rows, tile), scaled.astype(jnp.bfloat16),
                (((1,), (1,)), ((), ())), preferred_element_type=jnp.float32,
            )
            penalty = penalty + lax.dot_general(
                jnp.full((8, tile), 0.5, jnp.float32), scaled * refs_f,
                (((1,), (1,)), ((), ())), preferred_element_type=jnp.float32,
                precision=lax.Precision.HIGHEST,
            )
        scores = scores - penalty[0:1]
        S[src] = scores.reshape(R, rows, width)
        for k in masks:
            score_copy(src, k).start()

    own_image.wait()
    for k in order:
        arrived(X.at[peers[k]], x_rcv.at[peers[k]])
    score_chunk(b)

    gather_order = [0] + order

    def gather_step(dist, carry):
        below, above = b - dist, b + dist
        for k in gather_order:
            g = flipped(r, k, R)

            @pl.when(below >= 0)
            def _():
                arrived(PR.at[below, g], p_rcv.at[below, g])

                @pl.when(not_top)
                def _():
                    gather_copy(below, g, 1).start()

            @pl.when(above < B)
            def _():
                arrived(PR.at[above, g], p_rcv.at[above, g])

                @pl.when(not_bottom)
                def _():
                    gather_copy(above, g, -1).start()

        @pl.when(below >= 0)
        def _():
            score_chunk(below)

        @pl.when(above < B)
        def _():
            score_chunk(above)

        return carry

    lax.fori_loop(1, B, gather_step, 0)

    lane_group = lax.broadcasted_iota(jnp.int32, (rows, width), 1) // refs
    named = (routes[:, 0:1] == lane_group) | (routes[:, 1:2] == lane_group)
    chunks = []
    for c in range(B):
        total = S[c, r]
        for k in masks:
            arrived(SR.at[c, peers[k]], s_rcv.at[c, peers[k]])
            total = total + SR[c, peers[k]]
        chunks.append(jnp.where(named, total, -jnp.inf))
    highest = chunks[0]
    for c in range(1, B):
        highest = jnp.maximum(highest, chunks[c])
    highest = jnp.max(highest, axis=1, keepdims=True)
    spread = jnp.exp(chunks[0] - highest)
    for c in range(1, B):
        spread = spread + jnp.exp(chunks[c] - highest)
    normalizer = highest + jnp.log(jnp.sum(spread, axis=1, keepdims=True))
    for c in range(B):
        Q[c, r] = jnp.exp(chunks[c] - normalizer).astype(jnp.bfloat16)
    for k in masks:
        post_copy(k).start()
    norm[...] = jnp.broadcast_to(normalizer, norm.shape)
    for k in order:
        arrived(Q.at[:, peers[k]], q_rcv.at[peers[k]])

    def sum_chunk(d, dst):
        posterior = Q[d].reshape(R * rows, width)
        for t in range(Cs // tile):
            cut = pl.ds(t * tile, tile)
            product = lax.dot_general(
                posterior, X[:, :, cut].reshape(R * rows, tile),
                (((0,), (0,)), ((), ())), preferred_element_type=jnp.float32,
            )
            dst[d, :, :, cut] = product.reshape(R, refs, tile).astype(dst.dtype)

    reduce_order = masks + [0]

    def first_sums(step, carry):
        up, down = B - 1 - step, step

        @pl.when(b == 0)
        def _():
            sum_chunk(up, US)
            for k in reduce_order:
                up_copy(up, flipped(r, k, R)).start()

        @pl.when(b == B - 1)
        def _():
            sum_chunk(down, DS)
            for k in reduce_order:
                down_copy(down, flipped(r, k, R)).start()

        @pl.when((b > 0) & (up > b))
        def _():
            sum_chunk(up, PART)

        @pl.when((b < B - 1) & (down < b))
        def _():
            sum_chunk(down, PART)

        return carry

    lax.fori_loop(0, B - 1, first_sums, 0)
    sum_chunk(b, PART)

    def pass_on(step, carry):
        up, down = B - 1 - step, step
        for k in reduce_order:
            g = flipped(r, k, R)

            @pl.when((b > 0) & (up > b))
            def _():
                arrived(UR.at[up, g], u_rcv.at[up, g])
                US[up, g] = (PART[up, g] + UR[up, g].astype(jnp.float32)).astype(jnp.bfloat16)
                up_copy(up, g).start()

            @pl.when((b < B - 1) & (down < b))
            def _():
                arrived(DR.at[down, g], d_rcv.at[down, g])
                DS[down, g] = (PART[down, g] + DR[down, g].astype(jnp.float32)).astype(jnp.bfloat16)
                down_copy(down, g).start()

        return carry

    lax.fori_loop(0, B - 1, pass_on, 0)

    own_out = pltpu.make_async_copy(O.at[0], out.at[:, span(r)], loc.at[0])
    for k in reduce_order:
        g = flipped(r, k, R)

        @pl.when(not_bottom)
        def _():
            arrived(UR.at[b, g], u_rcv.at[b, g])
            PART[b, g] = PART[b, g] + UR[b, g].astype(jnp.float32)

        @pl.when(not_top)
        def _():
            arrived(DR.at[b, g], d_rcv.at[b, g])
            PART[b, g] = PART[b, g] + DR[b, g].astype(jnp.float32)

        O[k] = PART[b, g].astype(jnp.bfloat16)
        if k:
            out_copy(k).start()
        else:
            own_out.start()

    for k in masks:
        proj_copy(k).wait_send()
        image_copy(k).wait_send()
        post_copy(k).wait_send()

    def sent(i, carry):
        for k in masks:
            score_copy(i, k).wait_send()
        for g in range(R):
            @pl.when(not_top & (i <= b))
            def _():
                gather_copy(i, g, 1).wait_send()

            @pl.when(not_bottom & (i >= b))
            def _():
                gather_copy(i, g, -1).wait_send()

            @pl.when(i > b)
            def _():
                up_copy(i, g).wait_send()

            @pl.when(i < b)
            def _():
                down_copy(i, g).wait_send()

        return carry

    lax.fori_loop(0, B, sent, 0)
    own_out.wait()
    for k in masks:
        out_copy(k).wait_send()
        arrived(out.at[:, span(peers[k])], o_rcv.at[peers[k]])


def split_coefficients(images, routes, projections, noise_weights):
    R, B = lax.axis_size("reader"), lax.axis_size("blk")
    rows, coef = images.shape
    refs = projections.shape[1]
    Cs, width = coef // R, R * refs
    dma = pltpu.SemaphoreType.DMA
    bf16, f32 = jnp.bfloat16, jnp.float32
    sums, norm = pl.pallas_call(
        partial(kernel, R, B),
        out_shape=(
            jax.ShapeDtypeStruct((refs, coef), bf16),
            jax.ShapeDtypeStruct((rows, 128), f32),
        ),
        in_specs=[
            pl.BlockSpec(memory_space=pl.ANY),
            pl.BlockSpec(memory_space=pltpu.VMEM),
            pl.BlockSpec(memory_space=pl.ANY),
            pl.BlockSpec(memory_space=pltpu.VMEM),
        ],
        out_specs=(
            pl.BlockSpec(memory_space=pl.ANY),
            pl.BlockSpec(memory_space=pltpu.VMEM),
        ),
        scratch_shapes=[
            pltpu.VMEM((R, rows, Cs), bf16),
            pltpu.VMEM((B, R, refs, Cs), bf16),
            pltpu.VMEM((B, R, rows, width), f32),
            pltpu.VMEM((B, R, rows, width), f32),
            pltpu.VMEM((B, R, rows, width), bf16),
            pltpu.VMEM((B, R, refs, Cs), f32),
            pltpu.VMEM((B, R, refs, Cs), bf16),
            pltpu.VMEM((B, R, refs, Cs), bf16),
            pltpu.VMEM((B, R, refs, Cs), bf16),
            pltpu.VMEM((B, R, refs, Cs), bf16),
            pltpu.VMEM((R, refs, Cs), bf16),
            dma((2,)),
            dma((R,)), dma((B, R)), dma((R,)), dma((R,)),
            dma((B, R)), dma((B, R)),
            dma((B, R)), dma((B, R)),
            dma((R,)), dma((R,)),
            dma((B, R)), dma((B, R)), dma((B, R)), dma((B, R)),
            dma((R,)), dma((R,)),
        ],
        compiler_params=pltpu.CompilerParams(
            collective_id=0, has_side_effects=True, vmem_limit_bytes=50 * 1024 * 1024
        ),
        cost_estimate=pl.CostEstimate(
            flops=4 * R * rows * B * width * Cs, bytes_accessed=4 * rows * coef, transcendentals=0
        ),
    )(images, routes, projections[0], noise_weights.reshape(R, 1, Cs))
    return (sums.astype(f32)[None], norm[:, 0])


def solution(mesh):
    sizes = dict(mesh.shape)
    readers = sizes["reader"]
    direct = sizes["sub"] == 1 and readers > 1 and readers & (readers - 1) == 0
    return jax.shard_map(
        split_coefficients if direct else routed,
        mesh=mesh,
        in_specs=(
            P(("parts", "blk", "reader"), "sub"),
            P(("parts", "blk", "reader"), None),
            P(("parts", "reader"), "blk", "sub"),
            P(("parts", "sub")),
        ),
        out_specs=(P(("parts", "reader"), "blk", "sub"), P(("parts", "blk", "reader"))),
        check_vma=False,
    )
```

```python
from functools import partial

import jax
import jax.numpy as jnp
from jax import lax
from jax.experimental import pallas as pl
from jax.experimental.pallas import tpu as pltpu
from jax.sharding import PartitionSpec as P

MESH = pl.DeviceIdType.MESH


def from_behind(block, axis, distance):
    devices = range(lax.axis_size(axis))
    route = [((i - distance) % len(devices), i) for i in devices]
    return lax.ppermute(block, axis, route)


def slot_positions(route_block):
    flat = route_block.reshape(-1)
    order = jnp.arange(flat.shape[0], dtype=jnp.int32)
    earlier = (order[None, :] < order[:, None]) & (flat[None, :] == flat[:, None])
    return jnp.sum(earlier.astype(jnp.int32), axis=1).reshape(route_block.shape)


def combine_stats(row_peaks, row_totals):
    highest = jnp.max(row_peaks, axis=-1)
    spread = row_totals * jnp.exp(row_peaks - highest[..., None])
    return highest + jnp.log(jnp.sum(spread, axis=-1))


def routed(images, routes, projections, noise_weights):
    groups = lax.axis_size("reader")
    cycle_size = lax.axis_size("blk")
    my_group = lax.axis_index("reader")
    my_member = lax.axis_index("blk")
    per_device, top_count = routes.shape
    half_width = images.shape[1]
    capacity = min(per_device, 2 * per_device * top_count // groups)
    slot_count = groups * capacity
    ref_count = projections.shape[1]
    all_refs = ref_count * cycle_size
    anchor = jnp.zeros((), jnp.int32)
    own_index = slot_positions(routes)
    own_target = routes * capacity + own_index
    sources = jnp.broadcast_to(jnp.arange(per_device, dtype=jnp.int32)[:, None], routes.shape)
    picker = (
        jnp.full((slot_count,), per_device, jnp.int32)
        .at[own_target.reshape(-1)]
        .set(sources.reshape(-1))
    )
    padded = jnp.concatenate([images, jnp.zeros((1, half_width), images.dtype)], axis=0)
    outgoing = padded[picker].reshape(groups, capacity, half_width)
    received = lax.all_to_all(outgoing, "reader", split_axis=0, concat_axis=0, tiled=True).reshape(
        slot_count, half_width
    )
    every_route = lax.all_gather(routes, "reader", axis=0, tiled=True).reshape(
        groups, per_device, top_count
    )
    every_index = jax.vmap(slot_positions)(every_route)
    senders = jnp.arange(groups, dtype=jnp.int32)[:, None, None]
    landing = jnp.where(every_route == my_group, senders * capacity + every_index, slot_count)
    live_slot = jnp.zeros((slot_count,), jnp.int32).at[landing.reshape(-1)].set(1, mode="drop") > 0

    def score_block(ref_block):
        scaled = ref_block.astype(jnp.float32) * noise_weights[None, :]
        weighted = scaled.astype(jnp.bfloat16)
        penalty = 0.5 * jnp.sum(scaled * ref_block.astype(jnp.float32), axis=1)
        partial_scores = lax.dot_general(
            weighted, received, (((1,), (1,)), ((), ())), preferred_element_type=jnp.float32
        )
        return partial_scores - penalty[:, None]

    def cycle_turn(rotation, carry):
        ref_block, score_table = carry
        position = (my_member - rotation) % cycle_size
        score_table = lax.dynamic_update_slice(
            score_table, score_block(ref_block)[None], (position, anchor, anchor)
        )
        ref_block = from_behind(ref_block, "blk", 1)
        return (ref_block, score_table)

    empty_table = jnp.zeros((cycle_size, ref_count, slot_count), jnp.float32)
    ref_block, score_table = lax.fori_loop(
        0, cycle_size - 1, cycle_turn, (projections[0], empty_table)
    )
    position = (my_member + 1) % cycle_size
    score_table = lax.dynamic_update_slice(
        score_table, score_block(ref_block)[None], (position, anchor, anchor)
    )
    score_table = lax.psum(score_table, "sub")
    scores = score_table.reshape(all_refs, slot_count)
    row_peak = jnp.max(scores, axis=0)
    row_total = jnp.sum(jnp.exp(scores - row_peak[None, :]), axis=0)
    back_peak, back_total = (
        lax.all_to_all(
            row_peak.reshape(groups, capacity), "reader", split_axis=0, concat_axis=0, tiled=True
        ),
        lax.all_to_all(
            row_total.reshape(groups, capacity), "reader", split_axis=0, concat_axis=0, tiled=True
        ),
    )
    normalizer = combine_stats(
        back_peak.reshape(-1)[own_target], back_total.reshape(-1)[own_target]
    )
    outgoing_norm = (
        jnp.zeros((slot_count,), jnp.float32)
        .at[own_target.reshape(-1)]
        .set(jnp.repeat(normalizer, top_count))
    )
    slot_norm = lax.all_to_all(
        outgoing_norm.reshape(groups, capacity), "reader", split_axis=0, concat_axis=0, tiled=True
    ).reshape(slot_count)
    exponent = jnp.where(live_slot[None, :], scores - slot_norm[None, :], -jnp.inf)
    posterior = jnp.exp(exponent).astype(jnp.bfloat16)
    summed = lax.psum_scatter(
        jnp.dot(posterior, received, preferred_element_type=jnp.float32).astype(jnp.bfloat16),
        "blk",
        scatter_dimension=0,
        tiled=True,
    ).astype(jnp.float32)
    return (summed[None], normalizer)


def flipped(number, mask, size):
    result, bit = 0, 1
    while bit < size:
        digit = lax.rem(lax.div(number, bit), 2)
        result = result + bit * ((1 - digit) if mask & bit else digit)
        bit *= 2
    return result


def kernel(
    R, B,
    images, routes, proj, noise,
    out, norm,
    X, PR, S, SR, Q, PART, UR, DR, US, DS, O,
    loc, p_snd, p_rcv, x_snd, x_rcv, gu_snd, gd_snd, s_snd, s_rcv, q_snd, q_rcv,
    u_snd, u_rcv, d_snd, d_rcv, o_snd, o_rcv,
):
    r = lax.axis_index("reader")
    b = lax.axis_index("blk")
    rows = images.shape[0]
    refs = proj.shape[0]
    Cs = X.shape[2]
    T, tile = O.shape[0], O.shape[3]
    width = R * refs
    far = [k for k in range(R - 1, 1, -1)]
    masks = far + [1]
    peers = {k: flipped(r, k, R) for k in masks}
    not_top = b < B - 1
    not_bottom = b > 0

    def span(i):
        return pl.ds(pl.multiple_of(i * Cs, Cs), Cs)

    def to_reader(src, dst, snd, rcv, k):
        return pltpu.make_async_remote_copy(
            src_ref=src, dst_ref=dst, send_sem=snd, recv_sem=rcv,
            device_id={"reader": peers[k]}, device_id_type=MESH,
        )

    def to_blk(src, dst, snd, rcv, step):
        return pltpu.make_async_remote_copy(
            src_ref=src, dst_ref=dst, send_sem=snd, recv_sem=rcv,
            device_id={"blk": b + step}, device_id_type=MESH,
        )

    def proj_copy(k):
        return to_reader(proj.at[:, span(peers[k])], PR.at[b, r], p_snd.at[k], p_rcv.at[b, r], k)

    def image_copy(k):
        return to_reader(images.at[:, span(peers[k])], X.at[r], x_snd.at[k], x_rcv.at[r], k)

    def gather_copy(src, g, step):
        snd = gu_snd if step > 0 else gd_snd
        return to_blk(PR.at[src, g], PR.at[src, g], snd.at[src, g], p_rcv.at[src, g], step)

    def score_copy(src, k):
        return to_reader(S.at[src, peers[k]], SR.at[src, r], s_snd.at[src, k], s_rcv.at[src, r], k)

    def post_copy(k):
        return to_reader(Q.at[:, r], Q.at[:, r], q_snd.at[k], q_rcv.at[r], k)

    def up_copy(d, t):
        return to_blk(US.at[d, t], UR.at[d, t], u_snd.at[d, t], u_rcv.at[d, t], 1)

    def down_copy(d, t):
        return to_blk(DS.at[d, t], DR.at[d, t], d_snd.at[d, t], d_rcv.at[d, t], -1)

    def out_span(i, t):
        return out.at[:, pl.ds(pl.multiple_of(i * Cs + t * tile, tile), tile)]

    def out_copy(t, k):
        return to_reader(O.at[t, peers[k]], out_span(r, t), o_snd.at[t, k], o_rcv.at[t, r], k)

    def own_out(t):
        return pltpu.make_async_copy(O.at[t, r], out_span(r, t), o_snd.at[t, 0])

    def arrived(dst, sem):
        to_reader(dst, dst, sem, sem, 1).wait_recv()

    own_proj = pltpu.make_async_copy(proj.at[:, span(r)], PR.at[b, r], loc.at[0])
    own_image = pltpu.make_async_copy(images.at[:, span(r)], X.at[r], loc.at[1])
    own_proj.start()

    barrier = pltpu.get_barrier_semaphore()
    for k in masks:
        pl.semaphore_signal(barrier, inc=1, device_id={"reader": peers[k]}, device_id_type=MESH)

    @pl.when(not_top)
    def _():
        pl.semaphore_signal(barrier, inc=1, device_id={"blk": b + 1}, device_id_type=MESH)

    @pl.when(not_bottom)
    def _():
        pl.semaphore_signal(barrier, inc=1, device_id={"blk": b - 1}, device_id_type=MESH)

    pl.semaphore_wait(
        barrier, (R - 1) + not_top.astype(jnp.int32) + not_bottom.astype(jnp.int32)
    )

    for k in masks:
        proj_copy(k).start()
    own_proj.wait()

    def send_own(g):
        @pl.when(not_top)
        def _():
            gather_copy(b, g, 1).start()

        @pl.when(not_bottom)
        def _():
            gather_copy(b, g, -1).start()

    send_own(r)
    own_image.start()
    for k in masks:
        image_copy(k).start()
    order = [1] + far[::-1]
    for k in order:
        arrived(PR.at[b, peers[k]], p_rcv.at[b, peers[k]])
        send_own(peers[k])

    def score_chunk(src):
        scores = jnp.zeros((R * rows, width), jnp.float32)
        penalty = jnp.zeros((8, width), jnp.float32)
        for t in range(Cs // tile):
            cut = pl.ds(t * tile, tile)
            refs_f = PR[src, :, :, cut].reshape(width, tile).astype(jnp.float32)
            scaled = refs_f * noise[r, :, cut]
            scores = scores + lax.dot_general(
                X[:, :, cut].reshape(R * rows, tile), scaled.astype(jnp.bfloat16),
                (((1,), (1,)), ((), ())), preferred_element_type=jnp.float32,
            )
            penalty = penalty + lax.dot_general(
                jnp.full((8, tile), 0.5, jnp.float32), scaled * refs_f,
                (((1,), (1,)), ((), ())), preferred_element_type=jnp.float32,
                precision=lax.Precision.HIGHEST,
            )
        scores = scores - penalty[0:1]
        S[src] = scores.reshape(R, rows, width)
        for k in masks:
            score_copy(src, k).start()

    gather_order = [0] + order

    def forward(dist, carry):
        below, above = b - dist, b + dist
        for k in gather_order:
            g = flipped(r, k, R)

            @pl.when(below >= 0)
            def _():
                arrived(PR.at[below, g], p_rcv.at[below, g])

                @pl.when(not_top)
                def _():
                    gather_copy(below, g, 1).start()

            @pl.when(above < B)
            def _():
                arrived(PR.at[above, g], p_rcv.at[above, g])

                @pl.when(not_bottom)
                def _():
                    gather_copy(above, g, -1).start()

        return carry

    def score_pair(dist, carry):
        @pl.when(b - dist >= 0)
        def _():
            score_chunk(b - dist)

        @pl.when(b + dist < B)
        def _():
            score_chunk(b + dist)

        return carry

    lax.fori_loop(1, B - 1, forward, 0)
    own_image.wait()
    for k in order:
        arrived(X.at[peers[k]], x_rcv.at[peers[k]])
    score_chunk(b)
    lax.fori_loop(1, B - 1, score_pair, 0)
    forward(B - 1, 0)
    score_pair(B - 1, 0)

    lane_group = lax.broadcasted_iota(jnp.int32, (rows, width), 1) // refs
    named = (routes[:, 0:1] == lane_group) | (routes[:, 1:2] == lane_group)
    chunks = []
    for c in range(B):
        total = S[c, r]
        for k in masks:
            arrived(SR.at[c, peers[k]], s_rcv.at[c, peers[k]])
            total = total + SR[c, peers[k]]
        chunks.append(jnp.where(named, total, -jnp.inf))
    highest = chunks[0]
    for c in range(1, B):
        highest = jnp.maximum(highest, chunks[c])
    highest = jnp.max(highest, axis=1, keepdims=True)
    spread = jnp.exp(chunks[0] - highest)
    for c in range(1, B):
        spread = spread + jnp.exp(chunks[c] - highest)
    normalizer = highest + jnp.log(jnp.sum(spread, axis=1, keepdims=True))
    for c in range(B):
        Q[c, r] = jnp.exp(chunks[c] - normalizer).astype(jnp.bfloat16)
    for k in masks:
        post_copy(k).start()
    norm[...] = jnp.broadcast_to(normalizer, norm.shape)
    for k in order:
        arrived(Q.at[:, peers[k]], q_rcv.at[peers[k]])

    def product(d, t):
        return lax.dot_general(
            Q[d].reshape(R * rows, width), X[:, :, pl.ds(t * tile, tile)].reshape(R * rows, tile),
            (((0,), (0,)), ((), ())), preferred_element_type=jnp.float32,
        )

    def reduce_step(step, carry):
        up, down = B - 1 - step, step
        for t in range(T):
            @pl.when(b == 0)
            def _():
                US[up, t] = product(up, t).astype(jnp.bfloat16)
                up_copy(up, t).start()

            @pl.when(b == B - 1)
            def _():
                DS[down, t] = product(down, t).astype(jnp.bfloat16)
                down_copy(down, t).start()

            @pl.when((b > 0) & (up > b))
            def _():
                own = product(up, t)
                arrived(UR.at[up, t], u_rcv.at[up, t])
                US[up, t] = (own + UR[up, t].astype(jnp.float32)).astype(jnp.bfloat16)
                up_copy(up, t).start()

            @pl.when((b < B - 1) & (down < b))
            def _():
                own = product(down, t)
                arrived(DR.at[down, t], d_rcv.at[down, t])
                DS[down, t] = (own + DR[down, t].astype(jnp.float32)).astype(jnp.bfloat16)
                down_copy(down, t).start()

        return carry

    lax.fori_loop(0, B - 1, reduce_step, 0)

    for t in range(T):
        PART[t] = product(b, t)
    for t in range(T):
        @pl.when(not_bottom)
        def _():
            arrived(UR.at[b, t], u_rcv.at[b, t])
            PART[t] = PART[t] + UR[b, t].astype(jnp.float32)

        @pl.when(not_top)
        def _():
            arrived(DR.at[b, t], d_rcv.at[b, t])
            PART[t] = PART[t] + DR[b, t].astype(jnp.float32)

        O[t] = PART[t].reshape(R, refs, tile).astype(jnp.bfloat16)
        for k in masks:
            out_copy(t, k).start()
        own_out(t).start()

    for k in masks:
        proj_copy(k).wait_send()
        image_copy(k).wait_send()
        post_copy(k).wait_send()

    def sent(i, carry):
        for k in masks:
            score_copy(i, k).wait_send()
        for g in range(R):
            @pl.when(not_top & (i <= b))
            def _():
                gather_copy(i, g, 1).wait_send()

            @pl.when(not_bottom & (i >= b))
            def _():
                gather_copy(i, g, -1).wait_send()

        for t in range(T):
            @pl.when(i > b)
            def _():
                up_copy(i, t).wait_send()

            @pl.when(i < b)
            def _():
                down_copy(i, t).wait_send()

        return carry

    lax.fori_loop(0, B, sent, 0)
    for t in range(T):
        own_out(t).wait()
        for k in masks:
            out_copy(t, k).wait_send()
            arrived(out_span(peers[k], t), o_rcv.at[t, peers[k]])


def split_coefficients(images, routes, projections, noise_weights):
    R, B = lax.axis_size("reader"), lax.axis_size("blk")
    rows, coef = images.shape
    refs = projections.shape[1]
    Cs, width = coef // R, R * refs
    tile = min(Cs, 512)
    T = Cs // tile
    dma = pltpu.SemaphoreType.DMA
    bf16, f32 = jnp.bfloat16, jnp.float32
    sums, norm = pl.pallas_call(
        partial(kernel, R, B),
        out_shape=(
            jax.ShapeDtypeStruct((refs, coef), bf16),
            jax.ShapeDtypeStruct((rows, 128), f32),
        ),
        in_specs=[
            pl.BlockSpec(memory_space=pl.ANY),
            pl.BlockSpec(memory_space=pltpu.VMEM),
            pl.BlockSpec(memory_space=pl.ANY),
            pl.BlockSpec(memory_space=pltpu.VMEM),
        ],
        out_specs=(
            pl.BlockSpec(memory_space=pl.ANY),
            pl.BlockSpec(memory_space=pltpu.VMEM),
        ),
        scratch_shapes=[
            pltpu.VMEM((R, rows, Cs), bf16),
            pltpu.VMEM((B, R, refs, Cs), bf16),
            pltpu.VMEM((B, R, rows, width), f32),
            pltpu.VMEM((B, R, rows, width), f32),
            pltpu.VMEM((B, R, rows, width), bf16),
            pltpu.VMEM((T, width, tile), f32),
            pltpu.VMEM((B, T, width, tile), bf16),
            pltpu.VMEM((B, T, width, tile), bf16),
            pltpu.VMEM((B, T, width, tile), bf16),
            pltpu.VMEM((B, T, width, tile), bf16),
            pltpu.VMEM((T, R, refs, tile), bf16),
            dma((2,)),
            dma((R,)), dma((B, R)), dma((R,)), dma((R,)),
            dma((B, R)), dma((B, R)),
            dma((B, R)), dma((B, R)),
            dma((R,)), dma((R,)),
            dma((B, T)), dma((B, T)), dma((B, T)), dma((B, T)),
            dma((T, R)), dma((T, R)),
        ],
        compiler_params=pltpu.CompilerParams(
            collective_id=0, has_side_effects=True, vmem_limit_bytes=50 * 1024 * 1024
        ),
        cost_estimate=pl.CostEstimate(
            flops=4 * R * rows * B * width * Cs, bytes_accessed=4 * rows * coef, transcendentals=0
        ),
    )(images, routes, projections[0], noise_weights.reshape(R, 1, Cs))
    return (sums.astype(f32)[None], norm[:, 0])


def solution(mesh):
    sizes = dict(mesh.shape)
    readers = sizes["reader"]
    direct = sizes["sub"] == 1 and readers > 1 and readers & (readers - 1) == 0
    return jax.shard_map(
        split_coefficients if direct else routed,
        mesh=mesh,
        in_specs=(
            P(("parts", "blk", "reader"), "sub"),
            P(("parts", "blk", "reader"), None),
            P(("parts", "reader"), "blk", "sub"),
            P(("parts", "sub")),
        ),
        out_specs=(P(("parts", "reader"), "blk", "sub"), P(("parts", "blk", "reader"))),
        check_vma=False,
    )
```

```python
from functools import partial

import jax
import jax.numpy as jnp
from jax import lax
from jax.experimental import pallas as pl
from jax.experimental.pallas import tpu as pltpu
from jax.sharding import PartitionSpec as P

MESH = pl.DeviceIdType.MESH


def from_behind(block, axis, distance):
    devices = range(lax.axis_size(axis))
    route = [((i - distance) % len(devices), i) for i in devices]
    return lax.ppermute(block, axis, route)


def slot_positions(route_block):
    flat = route_block.reshape(-1)
    order = jnp.arange(flat.shape[0], dtype=jnp.int32)
    earlier = (order[None, :] < order[:, None]) & (flat[None, :] == flat[:, None])
    return jnp.sum(earlier.astype(jnp.int32), axis=1).reshape(route_block.shape)


def combine_stats(row_peaks, row_totals):
    highest = jnp.max(row_peaks, axis=-1)
    spread = row_totals * jnp.exp(row_peaks - highest[..., None])
    return highest + jnp.log(jnp.sum(spread, axis=-1))


def routed(images, routes, projections, noise_weights):
    groups = lax.axis_size("reader")
    cycle_size = lax.axis_size("blk")
    my_group = lax.axis_index("reader")
    my_member = lax.axis_index("blk")
    per_device, top_count = routes.shape
    half_width = images.shape[1]
    capacity = min(per_device, 2 * per_device * top_count // groups)
    slot_count = groups * capacity
    ref_count = projections.shape[1]
    all_refs = ref_count * cycle_size
    anchor = jnp.zeros((), jnp.int32)
    own_index = slot_positions(routes)
    own_target = routes * capacity + own_index
    sources = jnp.broadcast_to(jnp.arange(per_device, dtype=jnp.int32)[:, None], routes.shape)
    picker = (
        jnp.full((slot_count,), per_device, jnp.int32)
        .at[own_target.reshape(-1)]
        .set(sources.reshape(-1))
    )
    padded = jnp.concatenate([images, jnp.zeros((1, half_width), images.dtype)], axis=0)
    outgoing = padded[picker].reshape(groups, capacity, half_width)
    received = lax.all_to_all(outgoing, "reader", split_axis=0, concat_axis=0, tiled=True).reshape(
        slot_count, half_width
    )
    every_route = lax.all_gather(routes, "reader", axis=0, tiled=True).reshape(
        groups, per_device, top_count
    )
    every_index = jax.vmap(slot_positions)(every_route)
    senders = jnp.arange(groups, dtype=jnp.int32)[:, None, None]
    landing = jnp.where(every_route == my_group, senders * capacity + every_index, slot_count)
    live_slot = jnp.zeros((slot_count,), jnp.int32).at[landing.reshape(-1)].set(1, mode="drop") > 0

    def score_block(ref_block):
        scaled = ref_block.astype(jnp.float32) * noise_weights[None, :]
        weighted = scaled.astype(jnp.bfloat16)
        penalty = 0.5 * jnp.sum(scaled * ref_block.astype(jnp.float32), axis=1)
        partial_scores = lax.dot_general(
            weighted, received, (((1,), (1,)), ((), ())), preferred_element_type=jnp.float32
        )
        return partial_scores - penalty[:, None]

    def cycle_turn(rotation, carry):
        ref_block, score_table = carry
        position = (my_member - rotation) % cycle_size
        score_table = lax.dynamic_update_slice(
            score_table, score_block(ref_block)[None], (position, anchor, anchor)
        )
        ref_block = from_behind(ref_block, "blk", 1)
        return (ref_block, score_table)

    empty_table = jnp.zeros((cycle_size, ref_count, slot_count), jnp.float32)
    ref_block, score_table = lax.fori_loop(
        0, cycle_size - 1, cycle_turn, (projections[0], empty_table)
    )
    position = (my_member + 1) % cycle_size
    score_table = lax.dynamic_update_slice(
        score_table, score_block(ref_block)[None], (position, anchor, anchor)
    )
    score_table = lax.psum(score_table, "sub")
    scores = score_table.reshape(all_refs, slot_count)
    row_peak = jnp.max(scores, axis=0)
    row_total = jnp.sum(jnp.exp(scores - row_peak[None, :]), axis=0)
    back_peak, back_total = (
        lax.all_to_all(
            row_peak.reshape(groups, capacity), "reader", split_axis=0, concat_axis=0, tiled=True
        ),
        lax.all_to_all(
            row_total.reshape(groups, capacity), "reader", split_axis=0, concat_axis=0, tiled=True
        ),
    )
    normalizer = combine_stats(
        back_peak.reshape(-1)[own_target], back_total.reshape(-1)[own_target]
    )
    outgoing_norm = (
        jnp.zeros((slot_count,), jnp.float32)
        .at[own_target.reshape(-1)]
        .set(jnp.repeat(normalizer, top_count))
    )
    slot_norm = lax.all_to_all(
        outgoing_norm.reshape(groups, capacity), "reader", split_axis=0, concat_axis=0, tiled=True
    ).reshape(slot_count)
    exponent = jnp.where(live_slot[None, :], scores - slot_norm[None, :], -jnp.inf)
    posterior = jnp.exp(exponent).astype(jnp.bfloat16)
    summed = lax.psum_scatter(
        jnp.dot(posterior, received, preferred_element_type=jnp.float32).astype(jnp.bfloat16),
        "blk",
        scatter_dimension=0,
        tiled=True,
    ).astype(jnp.float32)
    return (summed[None], normalizer)


def flipped(number, mask, size):
    result, bit = 0, 1
    while bit < size:
        digit = lax.rem(lax.div(number, bit), 2)
        result = result + bit * ((1 - digit) if mask & bit else digit)
        bit *= 2
    return result


def kernel(
    R, B,
    images, routes_in, proj, noise_in,
    out, norm,
    routes, noise,
    X, PR, S, SR, Q, PART, UR, DR, US, DS, O,
    loc, p_snd, p_rcv, x_snd, x_rcv, gu_snd, gd_snd, s_snd, s_rcv, q_snd, q_rcv,
    u_snd, u_rcv, d_snd, d_rcv, o_snd, o_rcv,
):
    r = lax.axis_index("reader")
    b = lax.axis_index("blk")
    rows = images.shape[0]
    refs = proj.shape[0]
    Cs = X.shape[2]
    T, tile = O.shape[0], O.shape[3]
    width = R * refs
    far = [k for k in range(R - 1, 1, -1)]
    masks = far + [1]
    order = [1] + far[::-1]
    peers = {k: flipped(r, k, R) for k in masks}
    not_top = b < B - 1
    not_bottom = b > 0

    def span(i):
        return pl.ds(pl.multiple_of(i * Cs, Cs), Cs)

    def to_reader(src, dst, snd, rcv, k):
        return pltpu.make_async_remote_copy(
            src_ref=src, dst_ref=dst, send_sem=snd, recv_sem=rcv,
            device_id={"reader": peers[k]}, device_id_type=MESH,
        )

    def to_blk(src, dst, snd, rcv, step):
        return pltpu.make_async_remote_copy(
            src_ref=src, dst_ref=dst, send_sem=snd, recv_sem=rcv,
            device_id={"blk": b + step}, device_id_type=MESH,
        )

    def proj_copy(k):
        return to_reader(proj.at[:, span(peers[k])], PR.at[b, r], p_snd.at[k], p_rcv.at[b, r], k)

    def image_copy(k):
        return to_reader(images.at[:, span(peers[k])], X.at[r], x_snd.at[k], x_rcv.at[r], k)

    def gather_copy(src, g, step):
        snd = gu_snd if step > 0 else gd_snd
        return to_blk(PR.at[src, g], PR.at[src, g], snd.at[src, g], p_rcv.at[src, g], step)

    def score_copy(src, k):
        return to_reader(S.at[src, peers[k]], SR.at[src, r], s_snd.at[src, k], s_rcv.at[src, r], k)

    def post_copy(c, k):
        return to_reader(Q.at[c, r], Q.at[c, r], q_snd.at[c, k], q_rcv.at[c, r], k)

    def up_copy(d, t):
        return to_blk(US.at[d, t], UR.at[d, t], u_snd.at[d, t], u_rcv.at[d, t], 1)

    def down_copy(d, t):
        return to_blk(DS.at[d, t], DR.at[d, t], d_snd.at[d, t], d_rcv.at[d, t], -1)

    def out_span(i, t):
        return out.at[:, pl.ds(pl.multiple_of(i * Cs + t * tile, tile), tile)]

    def out_copy(t, k):
        return to_reader(O.at[t, peers[k]], out_span(r, t), o_snd.at[t, k], o_rcv.at[t, r], k)

    def own_out(t):
        return pltpu.make_async_copy(O.at[t, r], out_span(r, t), o_snd.at[t, 0])

    def arrived(dst, sem):
        to_reader(dst, dst, sem, sem, 1).wait_recv()

    own_proj = pltpu.make_async_copy(proj.at[:, span(r)], PR.at[b, r], loc.at[0])
    own_image = pltpu.make_async_copy(images.at[:, span(r)], X.at[r], loc.at[1])
    own_proj.start()
    noise_copy = pltpu.make_async_copy(noise_in, noise, loc.at[2])
    noise_copy.start()
    routes_copy = pltpu.make_async_copy(routes_in, routes, loc.at[3])
    routes_copy.start()

    barrier = pltpu.get_barrier_semaphore()
    for k in masks:
        pl.semaphore_signal(barrier, inc=1, device_id={"reader": peers[k]}, device_id_type=MESH)

    @pl.when(not_top)
    def _():
        pl.semaphore_signal(barrier, inc=1, device_id={"blk": b + 1}, device_id_type=MESH)

    @pl.when(not_bottom)
    def _():
        pl.semaphore_signal(barrier, inc=1, device_id={"blk": b - 1}, device_id_type=MESH)

    pl.semaphore_wait(
        barrier, (R - 1) + not_top.astype(jnp.int32) + not_bottom.astype(jnp.int32)
    )

    for k in order:
        proj_copy(k).start()
    own_proj.wait()

    def send_own(g):
        @pl.when(not_top)
        def _():
            gather_copy(b, g, 1).start()

        @pl.when(not_bottom)
        def _():
            gather_copy(b, g, -1).start()

    send_own(r)
    own_image.start()
    for k in masks:
        image_copy(k).start()
    for k in order:
        arrived(PR.at[b, peers[k]], p_rcv.at[b, peers[k]])
        send_own(peers[k])

    def score_chunk(src):
        scores = jnp.zeros((R * rows, width), jnp.float32)
        penalty = jnp.zeros((width, 128), jnp.float32)
        for t in range(Cs // tile):
            cut = pl.ds(t * tile, tile)
            refs_f = PR[src, :, :, cut].reshape(width, tile).astype(jnp.float32)
            weights = noise[pl.ds(pl.multiple_of(r * Cs + t * tile, tile), tile)]
            scaled = refs_f * weights[None, :]
            scores = scores + lax.dot_general(
                X[:, :, cut].reshape(R * rows, tile), scaled.astype(jnp.bfloat16),
                (((1,), (1,)), ((), ())), preferred_element_type=jnp.float32,
            )
            squares = scaled * refs_f
            for lane in range(0, tile, 128):
                penalty = penalty + squares[:, lane : lane + 128]
        penalty_row = lax.dot_general(
            jnp.full((8, 128), 0.5, jnp.float32), penalty,
            (((1,), (1,)), ((), ())), preferred_element_type=jnp.float32,
            precision=lax.Precision.HIGHEST,
        )
        scores = scores - penalty_row[0:1]
        S[src] = scores.reshape(R, rows, width)
        for k in masks:
            score_copy(src, k).start()

    gather_order = [0] + order

    def forward(dist, carry):
        below, above = b - dist, b + dist
        for k in gather_order:
            g = flipped(r, k, R)

            @pl.when(below >= 0)
            def _():
                arrived(PR.at[below, g], p_rcv.at[below, g])

                @pl.when(not_top)
                def _():
                    gather_copy(below, g, 1).start()

            @pl.when(above < B)
            def _():
                arrived(PR.at[above, g], p_rcv.at[above, g])

                @pl.when(not_bottom)
                def _():
                    gather_copy(above, g, -1).start()

        return carry

    def score_pair(dist, carry):
        @pl.when(b - dist >= 0)
        def _():
            score_chunk(b - dist)

        @pl.when(b + dist < B)
        def _():
            score_chunk(b + dist)

        return carry

    lax.fori_loop(1, B - 1, forward, 0)
    noise_copy.wait()
    routes_copy.wait()
    own_image.wait()
    for k in order:
        arrived(X.at[peers[k]], x_rcv.at[peers[k]])
    score_chunk(b)
    lax.fori_loop(1, B - 1, score_pair, 0)
    forward(B - 1, 0)
    score_pair(B - 1, 0)

    lane_group = lax.broadcasted_iota(jnp.int32, (rows, width), 1) // refs
    diagonal = lax.broadcasted_iota(jnp.int32, (rows, rows), 0) == lax.broadcasted_iota(
        jnp.int32, (rows, rows), 1
    )

    def column(row):
        return jnp.sum(jnp.where(diagonal, row, 0.0), axis=1, keepdims=True).astype(jnp.int32)

    names = routes[...].astype(jnp.float32)
    named = (column(names[0:1]) == lane_group) | (column(names[1:2]) == lane_group)
    chunks = []
    for c in range(B):
        total = S[c, r]
        for k in masks:
            arrived(SR.at[c, peers[k]], s_rcv.at[c, peers[k]])
            total = total + SR[c, peers[k]]
        chunks.append(jnp.where(named, total, -jnp.inf))
    highest = chunks[0]
    for c in range(1, B):
        highest = jnp.maximum(highest, chunks[c])
    highest = jnp.max(highest, axis=1, keepdims=True)
    spread = jnp.exp(chunks[0] - highest)
    for c in range(1, B):
        spread = spread + jnp.exp(chunks[c] - highest)
    normalizer = highest + jnp.log(jnp.sum(spread, axis=1, keepdims=True))
    for c in sorted(range(B), key=lambda c: min(c, B - 1 - c)):
        Q[c, r] = jnp.exp(chunks[c] - normalizer).astype(jnp.bfloat16)
        for k in masks:
            post_copy(c, k).start()
    norm[...] = jnp.broadcast_to(normalizer, norm.shape)
    def product(d, t):
        cut = pl.ds(pl.multiple_of(t * tile, tile), tile)
        return lax.dot_general(
            Q[d].reshape(R * rows, width), X[:, :, cut].reshape(R * rows, tile),
            (((0,), (0,)), ((), ())), preferred_element_type=jnp.float32,
        )

    def whole(d):
        for k in order:
            arrived(Q.at[d, peers[k]], q_rcv.at[d, peers[k]])

    pieces = (B - 1) * T

    def reduce_step(turn, carry):
        n = turn - b
        up, t = B - 1 - n // T, n % T

        @pl.when((n >= 0) & (n < pieces) & (up > b))
        def _():
            @pl.when(t == 0)
            def _():
                whole(up)

            own = product(up, t)

            @pl.when(b == 0)
            def _():
                US[up, t] = own.astype(jnp.bfloat16)

            @pl.when(b > 0)
            def _():
                arrived(UR.at[up, t], u_rcv.at[up, t])
                US[up, t] = (own + UR[up, t].astype(jnp.float32)).astype(jnp.bfloat16)

            up_copy(up, t).start()

        m = turn - (B - 1 - b)
        down, s = m // T, m % T

        @pl.when((m >= 0) & (m < pieces) & (down < b))
        def _():
            @pl.when(s == 0)
            def _():
                whole(down)

            own = product(down, s)

            @pl.when(b == B - 1)
            def _():
                DS[down, s] = own.astype(jnp.bfloat16)

            @pl.when(b < B - 1)
            def _():
                arrived(DR.at[down, s], d_rcv.at[down, s])
                DS[down, s] = (own + DR[down, s].astype(jnp.float32)).astype(jnp.bfloat16)

            down_copy(down, s).start()

        return carry

    lax.fori_loop(0, pieces + B - 1, reduce_step, 0)

    whole(b)
    for t in range(T):
        PART[t] = product(b, t)
    for t in range(T):
        @pl.when(not_bottom)
        def _():
            arrived(UR.at[b, t], u_rcv.at[b, t])
            PART[t] = PART[t] + UR[b, t].astype(jnp.float32)

        @pl.when(not_top)
        def _():
            arrived(DR.at[b, t], d_rcv.at[b, t])
            PART[t] = PART[t] + DR[b, t].astype(jnp.float32)

        O[t] = PART[t].reshape(R, refs, tile).astype(jnp.bfloat16)
        for k in masks:
            out_copy(t, k).start()
        own_out(t).start()

    for k in masks:
        proj_copy(k).wait_send()
        image_copy(k).wait_send()

    def sent(i, carry):
        for k in masks:
            score_copy(i, k).wait_send()
            post_copy(i, k).wait_send()
        for g in range(R):
            @pl.when(not_top & (i <= b))
            def _():
                gather_copy(i, g, 1).wait_send()

            @pl.when(not_bottom & (i >= b))
            def _():
                gather_copy(i, g, -1).wait_send()

        for t in range(T):
            @pl.when(i > b)
            def _():
                up_copy(i, t).wait_send()

            @pl.when(i < b)
            def _():
                down_copy(i, t).wait_send()

        return carry

    lax.fori_loop(0, B, sent, 0)
    for t in range(T):
        own_out(t).wait()
        for k in masks:
            out_copy(t, k).wait_send()
            arrived(out_span(peers[k], t), o_rcv.at[t, peers[k]])


def split_coefficients(images, routes, projections, noise_weights):
    R, B = lax.axis_size("reader"), lax.axis_size("blk")
    rows, coef = images.shape
    refs = projections.shape[1]
    Cs, width = coef // R, R * refs
    tile = min(Cs, 512)
    T = Cs // tile
    dma = pltpu.SemaphoreType.DMA
    bf16, f32 = jnp.bfloat16, jnp.float32
    sums, norm = pl.pallas_call(
        partial(kernel, R, B),
        out_shape=(
            jax.ShapeDtypeStruct((refs, coef), bf16),
            jax.ShapeDtypeStruct((rows, 128), f32),
        ),
        in_specs=[
            pl.BlockSpec(memory_space=pltpu.HBM),
            pl.BlockSpec(memory_space=pltpu.HBM),
            pl.BlockSpec(memory_space=pltpu.HBM),
            pl.BlockSpec(memory_space=pltpu.HBM),
        ],
        out_specs=(
            pl.BlockSpec(memory_space=pl.ANY),
            pl.BlockSpec(memory_space=pltpu.VMEM),
        ),
        scratch_shapes=[
            pltpu.VMEM((2, rows), jnp.int32),
            pltpu.VMEM((coef,), f32),
            pltpu.VMEM((R, rows, Cs), bf16),
            pltpu.VMEM((B, R, refs, Cs), bf16),
            pltpu.VMEM((B, R, rows, width), f32),
            pltpu.VMEM((B, R, rows, width), f32),
            pltpu.VMEM((B, R, rows, width), bf16),
            pltpu.VMEM((T, width, tile), f32),
            pltpu.VMEM((B, T, width, tile), bf16),
            pltpu.VMEM((B, T, width, tile), bf16),
            pltpu.VMEM((B, T, width, tile), bf16),
            pltpu.VMEM((B, T, width, tile), bf16),
            pltpu.VMEM((T, R, refs, tile), bf16),
            dma((4,)),
            dma((R,)), dma((B, R)), dma((R,)), dma((R,)),
            dma((B, R)), dma((B, R)),
            dma((B, R)), dma((B, R)),
            dma((B, R)), dma((B, R)),
            dma((B, T)), dma((B, T)), dma((B, T)), dma((B, T)),
            dma((T, R)), dma((T, R)),
        ],
        compiler_params=pltpu.CompilerParams(
            collective_id=0, has_side_effects=True, vmem_limit_bytes=64 * 1024 * 1024 - 65536
        ),
        cost_estimate=pl.CostEstimate(
            flops=4 * R * rows * B * width * Cs, bytes_accessed=4 * rows * coef, transcendentals=0
        ),
    )(images, routes.T, projections[0], noise_weights)
    return (sums.astype(f32)[None], norm[:, 0])


def solution(mesh):
    sizes = dict(mesh.shape)
    readers = sizes["reader"]
    direct = sizes["sub"] == 1 and readers > 1 and readers & (readers - 1) == 0
    return jax.shard_map(
        split_coefficients if direct else routed,
        mesh=mesh,
        in_specs=(
            P(("parts", "blk", "reader"), "sub"),
            P(("parts", "blk", "reader"), None),
            P(("parts", "reader"), "blk", "sub"),
            P(("parts", "sub")),
        ),
        out_specs=(P(("parts", "reader"), "blk", "sub"), P(("parts", "blk", "reader"))),
        check_vma=False,
    )
```

```python
from functools import partial

import jax
import jax.numpy as jnp
from jax import lax
from jax.experimental import pallas as pl
from jax.experimental.pallas import tpu as pltpu
from jax.sharding import PartitionSpec as P

MESH = pl.DeviceIdType.MESH


def from_behind(block, axis, distance):
    devices = range(lax.axis_size(axis))
    route = [((i - distance) % len(devices), i) for i in devices]
    return lax.ppermute(block, axis, route)


def slot_positions(route_block):
    flat = route_block.reshape(-1)
    order = jnp.arange(flat.shape[0], dtype=jnp.int32)
    earlier = (order[None, :] < order[:, None]) & (flat[None, :] == flat[:, None])
    return jnp.sum(earlier.astype(jnp.int32), axis=1).reshape(route_block.shape)


def combine_stats(row_peaks, row_totals):
    highest = jnp.max(row_peaks, axis=-1)
    spread = row_totals * jnp.exp(row_peaks - highest[..., None])
    return highest + jnp.log(jnp.sum(spread, axis=-1))


def routed(images, routes, projections, noise_weights):
    groups = lax.axis_size("reader")
    cycle_size = lax.axis_size("blk")
    my_group = lax.axis_index("reader")
    my_member = lax.axis_index("blk")
    per_device, top_count = routes.shape
    half_width = images.shape[1]
    capacity = min(per_device, 2 * per_device * top_count // groups)
    slot_count = groups * capacity
    ref_count = projections.shape[1]
    all_refs = ref_count * cycle_size
    anchor = jnp.zeros((), jnp.int32)
    own_index = slot_positions(routes)
    own_target = routes * capacity + own_index
    sources = jnp.broadcast_to(jnp.arange(per_device, dtype=jnp.int32)[:, None], routes.shape)
    picker = (
        jnp.full((slot_count,), per_device, jnp.int32)
        .at[own_target.reshape(-1)]
        .set(sources.reshape(-1))
    )
    padded = jnp.concatenate([images, jnp.zeros((1, half_width), images.dtype)], axis=0)
    outgoing = padded[picker].reshape(groups, capacity, half_width)
    received = lax.all_to_all(outgoing, "reader", split_axis=0, concat_axis=0, tiled=True).reshape(
        slot_count, half_width
    )
    every_route = lax.all_gather(routes, "reader", axis=0, tiled=True).reshape(
        groups, per_device, top_count
    )
    every_index = jax.vmap(slot_positions)(every_route)
    senders = jnp.arange(groups, dtype=jnp.int32)[:, None, None]
    landing = jnp.where(every_route == my_group, senders * capacity + every_index, slot_count)
    live_slot = jnp.zeros((slot_count,), jnp.int32).at[landing.reshape(-1)].set(1, mode="drop") > 0

    def score_block(ref_block):
        scaled = ref_block.astype(jnp.float32) * noise_weights[None, :]
        weighted = scaled.astype(jnp.bfloat16)
        penalty = 0.5 * jnp.sum(scaled * ref_block.astype(jnp.float32), axis=1)
        partial_scores = lax.dot_general(
            weighted, received, (((1,), (1,)), ((), ())), preferred_element_type=jnp.float32
        )
        return partial_scores - penalty[:, None]

    def cycle_turn(rotation, carry):
        ref_block, score_table = carry
        position = (my_member - rotation) % cycle_size
        score_table = lax.dynamic_update_slice(
            score_table, score_block(ref_block)[None], (position, anchor, anchor)
        )
        ref_block = from_behind(ref_block, "blk", 1)
        return (ref_block, score_table)

    empty_table = jnp.zeros((cycle_size, ref_count, slot_count), jnp.float32)
    ref_block, score_table = lax.fori_loop(
        0, cycle_size - 1, cycle_turn, (projections[0], empty_table)
    )
    position = (my_member + 1) % cycle_size
    score_table = lax.dynamic_update_slice(
        score_table, score_block(ref_block)[None], (position, anchor, anchor)
    )
    score_table = lax.psum(score_table, "sub")
    scores = score_table.reshape(all_refs, slot_count)
    row_peak = jnp.max(scores, axis=0)
    row_total = jnp.sum(jnp.exp(scores - row_peak[None, :]), axis=0)
    back_peak, back_total = (
        lax.all_to_all(
            row_peak.reshape(groups, capacity), "reader", split_axis=0, concat_axis=0, tiled=True
        ),
        lax.all_to_all(
            row_total.reshape(groups, capacity), "reader", split_axis=0, concat_axis=0, tiled=True
        ),
    )
    normalizer = combine_stats(
        back_peak.reshape(-1)[own_target], back_total.reshape(-1)[own_target]
    )
    outgoing_norm = (
        jnp.zeros((slot_count,), jnp.float32)
        .at[own_target.reshape(-1)]
        .set(jnp.repeat(normalizer, top_count))
    )
    slot_norm = lax.all_to_all(
        outgoing_norm.reshape(groups, capacity), "reader", split_axis=0, concat_axis=0, tiled=True
    ).reshape(slot_count)
    exponent = jnp.where(live_slot[None, :], scores - slot_norm[None, :], -jnp.inf)
    posterior = jnp.exp(exponent).astype(jnp.bfloat16)
    summed = lax.psum_scatter(
        jnp.dot(posterior, received, preferred_element_type=jnp.float32).astype(jnp.bfloat16),
        "blk",
        scatter_dimension=0,
        tiled=True,
    ).astype(jnp.float32)
    return (summed[None], normalizer)


def flipped(number, mask, size):
    result, bit = 0, 1
    while bit < size:
        digit = lax.rem(lax.div(number, bit), 2)
        result = result + bit * ((1 - digit) if mask & bit else digit)
        bit *= 2
    return result


def kernel(
    R, B,
    images, routes_in, proj, noise_in,
    out, norm,
    routes, noise,
    X, PR, S, SR, Q, PART, UR, DR, US, DS, O,
    loc, p_snd, p_rcv, x_snd, x_rcv, gu_snd, gd_snd, s_snd, s_rcv, q_snd, q_rcv,
    u_snd, u_rcv, d_snd, d_rcv, o_snd, o_rcv,
):
    r = lax.axis_index("reader")
    b = lax.axis_index("blk")
    rows = images.shape[0]
    refs = proj.shape[0]
    Cs = X.shape[2]
    T, tile = O.shape[0], O.shape[3]
    width = R * refs
    far = [k for k in range(R - 1, 1, -1)]
    masks = far + [1]
    order = [1] + far[::-1]
    peers = {k: flipped(r, k, R) for k in masks}
    not_top = b < B - 1
    not_bottom = b > 0

    def span(i):
        return pl.ds(pl.multiple_of(i * Cs, Cs), Cs)

    def to_reader(src, dst, snd, rcv, k):
        return pltpu.make_async_remote_copy(
            src_ref=src, dst_ref=dst, send_sem=snd, recv_sem=rcv,
            device_id={"reader": peers[k]}, device_id_type=MESH,
        )

    def to_blk(src, dst, snd, rcv, step):
        return pltpu.make_async_remote_copy(
            src_ref=src, dst_ref=dst, send_sem=snd, recv_sem=rcv,
            device_id={"blk": b + step}, device_id_type=MESH,
        )

    def proj_copy(k):
        return to_reader(proj.at[:, span(peers[k])], PR.at[b, r], p_snd.at[k], p_rcv.at[b, r], k)

    def image_copy(k):
        return to_reader(images.at[:, span(peers[k])], X.at[r], x_snd.at[k], x_rcv.at[r], k)

    def gather_copy(src, g, step):
        snd = gu_snd if step > 0 else gd_snd
        return to_blk(PR.at[src, g], PR.at[src, g], snd.at[src, g], p_rcv.at[src, g], step)

    def score_copy(src, k):
        return to_reader(S.at[src, peers[k]], SR.at[src, r], s_snd.at[src, k], s_rcv.at[src, r], k)

    def post_copy(c, k):
        return to_reader(Q.at[c, r], Q.at[c, r], q_snd.at[c, k], q_rcv.at[c, r], k)

    def up_copy(d, t):
        return to_blk(US.at[d, t], UR.at[d, t], u_snd.at[d, t], u_rcv.at[d, t], 1)

    def down_copy(d, t):
        return to_blk(DS.at[d, t], DR.at[d, t], d_snd.at[d, t], d_rcv.at[d, t], -1)

    def out_span(i, t):
        return out.at[:, pl.ds(pl.multiple_of(i * Cs + t * tile, tile), tile)]

    def out_copy(t, k):
        return to_reader(O.at[t, peers[k]], out_span(r, t), o_snd.at[t, k], o_rcv.at[t, r], k)

    def own_out(t):
        return pltpu.make_async_copy(O.at[t, r], out_span(r, t), o_snd.at[t, 0])

    def arrived(dst, sem):
        to_reader(dst, dst, sem, sem, 1).wait_recv()

    own_proj = pltpu.make_async_copy(proj.at[:, span(r)], PR.at[b, r], loc.at[0])
    own_image = pltpu.make_async_copy(images.at[:, span(r)], X.at[r], loc.at[1])
    own_proj.start()
    noise_copy = pltpu.make_async_copy(noise_in, noise, loc.at[2])
    noise_copy.start()
    routes_copy = pltpu.make_async_copy(routes_in, routes, loc.at[3])
    routes_copy.start()

    barrier = pltpu.get_barrier_semaphore()
    for k in masks:
        pl.semaphore_signal(barrier, inc=1, device_id={"reader": peers[k]}, device_id_type=MESH)

    @pl.when(not_top)
    def _():
        pl.semaphore_signal(barrier, inc=1, device_id={"blk": b + 1}, device_id_type=MESH)

    @pl.when(not_bottom)
    def _():
        pl.semaphore_signal(barrier, inc=1, device_id={"blk": b - 1}, device_id_type=MESH)

    pl.semaphore_wait(
        barrier, (R - 1) + not_top.astype(jnp.int32) + not_bottom.astype(jnp.int32)
    )

    for k in order:
        proj_copy(k).start()
    own_proj.wait()

    def send_own(g):
        @pl.when(not_top)
        def _():
            gather_copy(b, g, 1).start()

        @pl.when(not_bottom)
        def _():
            gather_copy(b, g, -1).start()

    send_own(r)
    own_image.start()
    for k in order:
        arrived(PR.at[b, peers[k]], p_rcv.at[b, peers[k]])
        send_own(peers[k])
    for k in masks:
        image_copy(k).start()

    def score_chunk(src):
        scores = jnp.zeros((R * rows, width), jnp.float32)
        penalty = jnp.zeros((width, 128), jnp.float32)
        for t in range(Cs // tile):
            cut = pl.ds(t * tile, tile)
            refs_f = PR[src, :, :, cut].reshape(width, tile).astype(jnp.float32)
            weights = noise[pl.ds(pl.multiple_of(r * Cs + t * tile, tile), tile)]
            scaled = refs_f * weights[None, :]
            scores = scores + lax.dot_general(
                X[:, :, cut].reshape(R * rows, tile), scaled.astype(jnp.bfloat16),
                (((1,), (1,)), ((), ())), preferred_element_type=jnp.float32,
            )
            squares = scaled * refs_f
            for lane in range(0, tile, 128):
                penalty = penalty + squares[:, lane : lane + 128]
        penalty_row = lax.dot_general(
            jnp.full((8, 128), 0.5, jnp.float32), penalty,
            (((1,), (1,)), ((), ())), preferred_element_type=jnp.float32,
            precision=lax.Precision.HIGHEST,
        )
        scores = scores - penalty_row[0:1]
        S[src] = scores.reshape(R, rows, width)
        for k in masks:
            score_copy(src, k).start()

    gather_order = [0] + order

    def forward(dist, carry):
        below, above = b - dist, b + dist
        for k in gather_order:
            g = flipped(r, k, R)

            @pl.when(below >= 0)
            def _():
                arrived(PR.at[below, g], p_rcv.at[below, g])

                @pl.when(not_top)
                def _():
                    gather_copy(below, g, 1).start()

            @pl.when(above < B)
            def _():
                arrived(PR.at[above, g], p_rcv.at[above, g])

                @pl.when(not_bottom)
                def _():
                    gather_copy(above, g, -1).start()

        return carry

    def score_pair(dist, carry):
        @pl.when(b - dist >= 0)
        def _():
            score_chunk(b - dist)

        @pl.when(b + dist < B)
        def _():
            score_chunk(b + dist)

        return carry

    lax.fori_loop(1, B - 1, forward, 0)
    noise_copy.wait()
    routes_copy.wait()
    own_image.wait()
    for k in order:
        arrived(X.at[peers[k]], x_rcv.at[peers[k]])
    score_chunk(b)
    lax.fori_loop(1, B - 1, score_pair, 0)
    forward(B - 1, 0)
    score_pair(B - 1, 0)

    lane_group = lax.broadcasted_iota(jnp.int32, (rows, width), 1) // refs
    diagonal = lax.broadcasted_iota(jnp.int32, (rows, rows), 0) == lax.broadcasted_iota(
        jnp.int32, (rows, rows), 1
    )

    def column(row):
        return jnp.sum(jnp.where(diagonal, row, 0.0), axis=1, keepdims=True).astype(jnp.int32)

    names = routes[...].astype(jnp.float32)
    named = (column(names[0:1]) == lane_group) | (column(names[1:2]) == lane_group)
    chunks = []
    for c in range(B):
        total = S[c, r]
        for k in masks:
            arrived(SR.at[c, peers[k]], s_rcv.at[c, peers[k]])
            total = total + SR[c, peers[k]]
        chunks.append(jnp.where(named, total, -jnp.inf))
    highest = chunks[0]
    for c in range(1, B):
        highest = jnp.maximum(highest, chunks[c])
    highest = jnp.max(highest, axis=1, keepdims=True)
    spread = jnp.exp(chunks[0] - highest)
    for c in range(1, B):
        spread = spread + jnp.exp(chunks[c] - highest)
    normalizer = highest + jnp.log(jnp.sum(spread, axis=1, keepdims=True))
    for c in range(B):
        Q[c, r] = jnp.exp(chunks[c] - normalizer).astype(jnp.bfloat16)
    lower = (2 * b < B).astype(jnp.int32)
    for i in range(B):
        for k in masks:
            post_copy(i + lower * (B - 1 - 2 * i), k).start()
    norm[...] = jnp.broadcast_to(normalizer, norm.shape)
    def product(d, t):
        cut = pl.ds(pl.multiple_of(t * tile, tile), tile)
        return lax.dot_general(
            Q[d].reshape(R * rows, width), X[:, :, cut].reshape(R * rows, tile),
            (((0,), (0,)), ((), ())), preferred_element_type=jnp.float32,
        )

    def whole(d):
        for k in order:
            arrived(Q.at[d, peers[k]], q_rcv.at[d, peers[k]])

    pieces = (B - 1) * T

    def reduce_step(turn, carry):
        n = turn - b
        up, t = B - 1 - n // T, n % T

        @pl.when((n >= 0) & (n < pieces) & (up > b))
        def _():
            @pl.when(t == 0)
            def _():
                whole(up)

            own = product(up, t)

            @pl.when(b == 0)
            def _():
                US[up, t] = own.astype(jnp.bfloat16)

            @pl.when(b > 0)
            def _():
                arrived(UR.at[up, t], u_rcv.at[up, t])
                US[up, t] = (own + UR[up, t].astype(jnp.float32)).astype(jnp.bfloat16)

            up_copy(up, t).start()

        m = turn - (B - 1 - b)
        down, s = m // T, m % T

        @pl.when((m >= 0) & (m < pieces) & (down < b))
        def _():
            @pl.when(s == 0)
            def _():
                whole(down)

            own = product(down, s)

            @pl.when(b == B - 1)
            def _():
                DS[down, s] = own.astype(jnp.bfloat16)

            @pl.when(b < B - 1)
            def _():
                arrived(DR.at[down, s], d_rcv.at[down, s])
                DS[down, s] = (own + DR[down, s].astype(jnp.float32)).astype(jnp.bfloat16)

            down_copy(down, s).start()

        return carry

    lax.fori_loop(0, pieces + B - 1, reduce_step, 0)

    whole(b)
    for t in range(T):
        PART[t] = product(b, t)
    for t in range(T):
        @pl.when(not_bottom)
        def _():
            arrived(UR.at[b, t], u_rcv.at[b, t])
            PART[t] = PART[t] + UR[b, t].astype(jnp.float32)

        @pl.when(not_top)
        def _():
            arrived(DR.at[b, t], d_rcv.at[b, t])
            PART[t] = PART[t] + DR[b, t].astype(jnp.float32)

        O[t] = PART[t].reshape(R, refs, tile).astype(jnp.bfloat16)
        for k in masks:
            out_copy(t, k).start()
        own_out(t).start()

    for k in masks:
        proj_copy(k).wait_send()
        image_copy(k).wait_send()

    def sent(i, carry):
        for k in masks:
            score_copy(i, k).wait_send()
            post_copy(i, k).wait_send()
        for g in range(R):
            @pl.when(not_top & (i <= b))
            def _():
                gather_copy(i, g, 1).wait_send()

            @pl.when(not_bottom & (i >= b))
            def _():
                gather_copy(i, g, -1).wait_send()

        for t in range(T):
            @pl.when(i > b)
            def _():
                up_copy(i, t).wait_send()

            @pl.when(i < b)
            def _():
                down_copy(i, t).wait_send()

        return carry

    lax.fori_loop(0, B, sent, 0)
    for t in range(T):
        own_out(t).wait()
        for k in masks:
            out_copy(t, k).wait_send()
            arrived(out_span(peers[k], t), o_rcv.at[t, peers[k]])


def split_coefficients(images, routes, projections, noise_weights):
    R, B = lax.axis_size("reader"), lax.axis_size("blk")
    rows, coef = images.shape
    refs = projections.shape[1]
    Cs, width = coef // R, R * refs
    tile = min(Cs, 512)
    T = Cs // tile
    dma = pltpu.SemaphoreType.DMA
    bf16, f32 = jnp.bfloat16, jnp.float32
    sums, norm = pl.pallas_call(
        partial(kernel, R, B),
        out_shape=(
            jax.ShapeDtypeStruct((refs, coef), bf16),
            jax.ShapeDtypeStruct((rows, 128), f32),
        ),
        in_specs=[
            pl.BlockSpec(memory_space=pltpu.HBM),
            pl.BlockSpec(memory_space=pltpu.HBM),
            pl.BlockSpec(memory_space=pltpu.HBM),
            pl.BlockSpec(memory_space=pltpu.HBM),
        ],
        out_specs=(
            pl.BlockSpec(memory_space=pl.ANY),
            pl.BlockSpec(memory_space=pltpu.VMEM),
        ),
        scratch_shapes=[
            pltpu.VMEM((2, rows), jnp.int32),
            pltpu.VMEM((coef,), f32),
            pltpu.VMEM((R, rows, Cs), bf16),
            pltpu.VMEM((B, R, refs, Cs), bf16),
            pltpu.VMEM((B, R, rows, width), f32),
            pltpu.VMEM((B, R, rows, width), f32),
            pltpu.VMEM((B, R, rows, width), bf16),
            pltpu.VMEM((T, width, tile), f32),
            pltpu.VMEM((B, T, width, tile), bf16),
            pltpu.VMEM((B, T, width, tile), bf16),
            pltpu.VMEM((B, T, width, tile), bf16),
            pltpu.VMEM((B, T, width, tile), bf16),
            pltpu.VMEM((T, R, refs, tile), bf16),
            dma((4,)),
            dma((R,)), dma((B, R)), dma((R,)), dma((R,)),
            dma((B, R)), dma((B, R)),
            dma((B, R)), dma((B, R)),
            dma((B, R)), dma((B, R)),
            dma((B, T)), dma((B, T)), dma((B, T)), dma((B, T)),
            dma((T, R)), dma((T, R)),
        ],
        compiler_params=pltpu.CompilerParams(
            collective_id=0, has_side_effects=True, vmem_limit_bytes=64 * 1024 * 1024 - 65536
        ),
        cost_estimate=pl.CostEstimate(
            flops=4 * R * rows * B * width * Cs, bytes_accessed=4 * rows * coef, transcendentals=0
        ),
    )(images, routes.T, projections[0], noise_weights)
    return (sums.astype(f32)[None], norm[:, 0])


def solution(mesh):
    sizes = dict(mesh.shape)
    readers = sizes["reader"]
    direct = sizes["sub"] == 1 and readers > 1 and readers & (readers - 1) == 0
    return jax.shard_map(
        split_coefficients if direct else routed,
        mesh=mesh,
        in_specs=(
            P(("parts", "blk", "reader"), "sub"),
            P(("parts", "blk", "reader"), None),
            P(("parts", "reader"), "blk", "sub"),
            P(("parts", "sub")),
        ),
        out_specs=(P(("parts", "reader"), "blk", "sub"), P(("parts", "blk", "reader"))),
        check_vma=False,
    )
```
